256 devices in a mesh: seq: 4 (over z_hi), vocab: 64 (over y, x, z_lo, core).
Axes of the slice: x: 4, y: 4, z: 8 (z_hi: 4, z_lo: 2; z = z_hi * 2 + z_lo), core: 2. Of those that a mesh axis runs over, the one named last changes fastest.
Arguments:
- student_hidden: bfloat16 [2048, 4096], P('seq')
- head_weight: bfloat16 [4096, 81920], P(None, 'vocab'), may hold values from -0.09375 to 0.09375
- teacher_logprob: bfloat16 [2048, 81920], P(('seq', 'vocab')), may hold values from -16 to 16
- lengths: int32 [8], P('seq'), may hold values from 1 to 256, as said below
Outputs:
- hidden_grad: bfloat16 [2048, 4096], P(('seq', 'vocab'))
- token_kl: float32 [2048], P(('seq', 'vocab'))
The draws below stay inside these ranges and needn't reach their ends.
Inputs may be any that keep to these rules, and one draw needn't show every extreme that they name: `lengths`: each sequence length lies in 1 to 256, and in every draw some sequence has length exactly 256.
All inputs are finite; a program needn't handle non-finite values.
Results may differ from the reference program's by a relative error of at most 0.0065.
Values may be sent and summed in bfloat16 or wider, within the bound.
No kernel may reach another device: no remote copies, remote signals or barrier semaphores. Data moves between devices by JAX's collectives and lax.ppermute only.
A program may use at most 128 MiB of HBM per device.

```python
import jax
import jax.numpy as jnp
from jax import lax

D = 4096
SEQ_LEN = 256
SEQS = 8
TOKENS = 2048
V = 81920


def draw_student_hidden(key, part):
    key = jax.random.fold_in(key, 11)
    first = jax.random.fold_in(key, 0)
    values = jax.random.normal(first, (TOKENS, D), jnp.float32) * 3.0
    return values.astype(jnp.bfloat16)


def draw_lengths(key, part):
    key = jax.random.fold_in(key, 23)
    first, second = jax.random.split(key, 2)
    drawn = jax.random.randint(first, (SEQS,), 1, SEQ_LEN + 1).astype(jnp.int32)
    chosen = jax.random.randint(second, (), 0, SEQS).astype(jnp.int32)
    position = jnp.arange(SEQS).astype(jnp.int32)
    return jnp.where(position == chosen, jnp.int32(SEQ_LEN), drawn).astype(jnp.int32)


def level_of(stream_key, dims, cuts, least, top_value):
    level = 1.0
    for dim, blocks in cuts:
        steps = jax.random.uniform(jax.random.fold_in(jax.random.fold_in(stream_key, 6), dim), (blocks,), jnp.float32, least / len(cuts), top_value / len(cuts))
        level = level * jnp.repeat(jnp.exp(steps), dims[dim] // blocks).reshape((-1,) + (1,) * (len(dims) - 1 - dim))
    return level


def normal_values(key, dims, deviation, bound, cuts=(), held_as=jnp.bfloat16):
    factor_of = level_of(key, dims, cuts, -0.22, 0.18) if cuts else 1.0
    values = jax.random.normal(key, dims, jnp.float32) * deviation * factor_of
    return jnp.minimum(jnp.maximum(values, -bound), bound).astype(held_as)


def setup_inputs(seed: int = 0) -> dict:
    key_list = jax.random.split(jax.random.key(seed), 5)
    student_hidden = draw_student_hidden(jax.random.fold_in(key_list[4], 71), 0)
    head_weight = normal_values(key_list[1], (D, V), D ** -0.5, 0.09375, ((1, 64),))
    teacher_logprob = normal_values(key_list[2], (TOKENS, V), 3.0, 16.0, ((0, 256),))
    lengths = draw_lengths(jax.random.fold_in(key_list[4], 71), 0)
    return {"student_hidden": student_hidden, "head_weight": head_weight, "teacher_logprob": teacher_logprob, "lengths": lengths}


def reference(student_hidden, head_weight, teacher_logprob, lengths):
    logits = jnp.dot(student_hidden, head_weight, preferred_element_type=jnp.float32)
    top = jnp.max(logits, axis=1)
    total = jnp.sum(jnp.exp(logits - top[:, None]), axis=1)
    lse = top + jnp.log(total)
    probs = jnp.exp(logits - lse[:, None])
    advantage = logits - lse[:, None] - teacher_logprob.astype(jnp.float32)
    expect = jnp.sum(probs * advantage, axis=1)
    live = (jnp.arange(SEQ_LEN)[None, :] < lengths[:, None]).reshape(TOKENS).astype(jnp.float32)
    count = jnp.sum(lengths).astype(jnp.float32)
    weight = live * (float(TOKENS) / count)
    grad = (weight[:, None] * probs * (advantage - expect[:, None])).astype(jnp.bfloat16)
    hidden_grad = lax.dot_general(grad, head_weight, (((1,), (1,)), ((), ())), preferred_element_type=jnp.float32)
    return hidden_grad.astype(jnp.bfloat16), live * expect
```

```python
import jax
import jax.numpy as jnp
from jax import lax
from jax.sharding import Mesh, PartitionSpec as P

VOCAB = ("y", "x", "z", "core")
CHIPS = ("y", "x", "z")
F32 = jnp.float32
BF16 = jnp.bfloat16


def body(student_hidden, head_weight, teacher_logprob, lengths):
    rows, depth = student_hidden.shape
    width = head_weight.shape[1]
    seq_count = lengths.shape[0]
    slot_count = rows // seq_count
    devices = lax.axis_size(VOCAB)
    chips = devices // 2
    own_rows = rows // devices
    seq_devices = lax.axis_size("seq")
    core = lax.axis_index("core")
    place = lax.axis_index(VOCAB)

    teacher = lax.all_to_all(teacher_logprob, VOCAB, split_axis=1, concat_axis=0, tiled=True)
    logits = jnp.dot(student_hidden, head_weight, preferred_element_type=F32)
    top = jnp.max(logits, axis=1)
    total = jnp.sum(jnp.exp(logits - top[:, None]), axis=1)

    count = jnp.sum(lengths).astype(F32).reshape(1, 1)
    count = count + sum(
        lax.ppermute(count, "seq", [(i, (i + d) % seq_devices) for i in range(seq_devices)])
        for d in range(1, seq_devices)
    )
    count = count[0, 0]

    shifted = logits - top[:, None]
    part = jnp.sum(jnp.exp(shifted) * (shifted - teacher.astype(F32)), axis=1)
    stats = jnp.stack([top, total, part])
    stats = jnp.broadcast_to(stats[None], (devices,) + stats.shape)
    stats = lax.all_to_all(stats, VOCAB, split_axis=0, concat_axis=0, tiled=True)
    tops, totals, parts = stats[:, 0], stats[:, 1], stats[:, 2]
    high = jnp.max(tops, axis=0)
    scale = jnp.exp(tops - high[None])
    whole = jnp.sum(totals * scale, axis=0)
    lse = high + jnp.log(whole)
    expect = jnp.sum(scale * (parts + totals * (tops - lse[None])), axis=0) / whole

    cut = (chips, 2, own_rows)

    def grad_of(which):
        def pick(value):
            value = value.reshape(cut + value.shape[1:])
            return lax.dynamic_index_in_dim(value, which, 1, keepdims=False)

        score = pick(logits) - pick(lse)[..., None]
        gap = score - pick(teacher).astype(F32) - pick(expect)[..., None]
        grad = (jnp.exp(score) * gap).astype(BF16)
        return lax.dot_general(
            grad.reshape(rows // 2, width),
            head_weight,
            (((1,), (1,)), ((), ())),
            preferred_element_type=F32,
        )

    away = grad_of(1 - core).astype(BF16)
    arrived = lax.ppermute(away, "core", [(0, 1), (1, 0)])
    chip_sum = (grad_of(core) + arrived.astype(F32)).astype(BF16)
    spread = lax.all_to_all(
        chip_sum.reshape(chips, own_rows, depth), CHIPS, split_axis=0, concat_axis=0, tiled=True
    )
    summed = jnp.sum(spread.astype(F32), axis=0)

    start = place * own_rows
    slots = start + jnp.arange(own_rows)
    live = (slots % slot_count < lengths[slots // slot_count]).astype(F32)
    weight = live * (float(rows * seq_devices) / count)
    hidden_grad = (weight[:, None] * summed).astype(BF16)
    token_kl = live * lax.dynamic_slice_in_dim(expect, start, own_rows, 0)
    return hidden_grad, token_kl


def solution(mesh):
    fine = Mesh(mesh.devices.reshape(4, 4, 4, 2, 2), ("seq",) + VOCAB)
    both = ("seq",) + VOCAB
    return jax.shard_map(
        body,
        mesh=fine,
        in_specs=(P("seq", None), P(None, VOCAB), P(both, None), P("seq")),
        out_specs=(P(both, None), P(both)),
        check_vma=False,
    )
```

```python
import jax
import jax.numpy as jnp
from jax import lax
from jax.experimental import pallas as pl
from jax.experimental.pallas import tpu as pltpu
from jax.sharding import Mesh, PartitionSpec as P

VOCAB = ("y", "x", "z", "core")
CHIPS = ("y", "x", "z")
ALL = ("seq",) + VOCAB
F32 = jnp.float32
BF16 = jnp.bfloat16
STEP = 512


def half_product(left, weight, which, out_type):
    rows, width = left.shape
    half = weight.shape[0] // 2
    step = min(STEP, half)
    steps = half // step

    def kernel(which_ref, left_ref, weight_ref, out_ref):
        out_ref[...] = lax.dot_general(
            left_ref[...],
            weight_ref[...],
            (((1,), (1,)), ((), ())),
            preferred_element_type=F32,
        ).astype(out_ref.dtype)

    return pl.pallas_call(
        kernel,
        out_shape=jax.ShapeDtypeStruct((rows, half), out_type),
        grid_spec=pltpu.PrefetchScalarGridSpec(
            num_scalar_prefetch=1,
            grid=(steps,),
            in_specs=[
                pl.BlockSpec((rows, width), lambda i, w: (0, 0)),
                pl.BlockSpec((step, width), lambda i, w: (w[0] * steps + i, 0)),
            ],
            out_specs=pl.BlockSpec((rows, step), lambda i, w: (0, i)),
        ),
        compiler_params=pltpu.CompilerParams(vmem_limit_bytes=24 * 2**20),
        cost_estimate=pl.CostEstimate(
            flops=2 * rows * width * half,
            bytes_accessed=2 * (rows * width + half * width + rows * half),
            transcendentals=0,
        ),
    )(which, left, weight)


def body(student_hidden, head_weight, teacher_logprob, lengths):
    rows, depth = student_hidden.shape
    seq_count = lengths.shape[0]
    slot_count = rows // seq_count
    devices = lax.axis_size(VOCAB)
    chips = devices // 2
    own_rows = rows // devices
    chip_rows = 2 * own_rows
    seq_devices = lax.axis_size("seq")
    core = lax.axis_index("core")
    place = lax.axis_index(VOCAB)
    mine = core.astype(jnp.int32).reshape(1)
    other = 1 - mine

    def swap(value):
        return lax.ppermute(value, "core", [(0, 1), (1, 0)])

    count = jnp.sum(lengths).astype(F32).reshape(1, 1)
    block = devices // lax.axis_size("y")
    heard = lax.ppermute(
        count,
        ALL,
        [
            (s * devices + v, (s + v // block) % seq_devices * devices + v)
            for s in range(seq_devices)
            for v in range(devices)
        ],
    )

    teacher = lax.all_to_all(teacher_logprob, VOCAB, split_axis=1, concat_axis=0, tiled=True)
    logits = jnp.dot(student_hidden, head_weight, preferred_element_type=F32)
    top = jnp.max(logits, axis=1)
    shifted = logits - top[:, None]
    mass = jnp.exp(shifted)
    total = jnp.sum(mass, axis=1)
    mass_half = mass.astype(BF16)
    base_away = swap(half_product(mass_half, head_weight, other, BF16))
    base = half_product(mass_half, head_weight, mine, BF16)

    advantage = shifted - teacher.astype(F32)
    part = jnp.sum(mass * advantage, axis=1)
    mean = part / total
    grad = (mass * (advantage - mean[:, None])).astype(BF16)

    stats = jnp.stack([top, total, mean, jnp.broadcast_to(heard[0], (rows,))])
    stats = jnp.broadcast_to(stats[None], (devices,) + stats.shape)
    stats = lax.all_to_all(stats, VOCAB, split_axis=0, concat_axis=0, tiled=True)

    slope_away = swap(half_product(grad, head_weight, other, BF16))
    slope = half_product(grad, head_weight, mine, F32)

    tops, totals, means = stats[:, 0], stats[:, 1], stats[:, 2]
    high = jnp.max(tops, axis=0)
    scale = jnp.exp(tops - high[None])
    whole = jnp.sum(totals * scale, axis=0)
    lse = high + jnp.log(whole)
    levels = means + (tops - lse[None])
    expect = jnp.sum(scale * totals * levels, axis=0) / whole
    count = jnp.sum(stats[:, 3, 0]) * (float(seq_devices) / float(devices))

    def merge(slope, base, stat):
        factor = jnp.exp(stat[0] - lse)
        offset = stat[2] + (stat[0] - lse) - expect
        return factor[:, None] * (slope.astype(F32) + offset[:, None] * base.astype(F32))

    sibling = lax.dynamic_index_in_dim(stats, place + 1 - 2 * core, 0, keepdims=False)
    near = jnp.stack([top, total, mean])
    chip_sum = (merge(slope, base, near) + merge(slope_away, base_away, sibling)).astype(BF16)
    spread = lax.all_to_all(
        chip_sum.reshape(chips, chip_rows, depth // 2),
        CHIPS,
        split_axis=0,
        concat_axis=0,
        tiled=True,
    )
    summed = jnp.sum(spread.astype(F32), axis=0)

    start = (place - core) * own_rows
    slots = start + jnp.arange(chip_rows)
    live = slots % slot_count < jnp.repeat(lengths, slot_count)[slots]
    live = live.astype(F32)
    weight = live * (float(rows * seq_devices) / count)
    rounded = (weight[:, None] * summed).astype(BF16)
    keep = lax.dynamic_slice_in_dim(rounded, core * own_rows, own_rows, 0)
    give = lax.dynamic_slice_in_dim(rounded, (1 - core) * own_rows, own_rows, 0)
    get = swap(give)
    hidden_grad = jnp.where(
        core == 0,
        jnp.concatenate([keep, get], axis=1),
        jnp.concatenate([get, keep], axis=1),
    )
    chip_kl = live * lax.dynamic_slice_in_dim(expect, start, chip_rows, 0)
    token_kl = lax.dynamic_slice_in_dim(chip_kl, core * own_rows, own_rows, 0)
    return hidden_grad, token_kl


def split_mesh(mesh, sizes):
    return Mesh(mesh.devices.reshape(sizes), ALL)


def solution(mesh, sizes=(4, 4, 4, 2, 2)):
    return jax.shard_map(
        body,
        mesh=split_mesh(mesh, sizes),
        in_specs=(P("seq", None), P(None, VOCAB), P(ALL, None), P("seq")),
        out_specs=(P(ALL, None), P(ALL)),
        check_vma=False,
    )
```

```python
import jax
import jax.numpy as jnp
from jax import lax
from jax.experimental import pallas as pl
from jax.experimental.pallas import tpu as pltpu
from jax.sharding import Mesh, PartitionSpec as P

VOCAB = ("y", "x", "z", "core")
ALL = ("seq",) + VOCAB
F32 = jnp.float32
BF16 = jnp.bfloat16
MIB = 2**20
LANES = 128
ACROSS = (((1,), (1,)), ((), ()))


def place_of(memory):
    return pl.BlockSpec(memory_space=memory)


VMEM = place_of(pltpu.VMEM)
HBM = place_of(pltpu.HBM)
SMEM = place_of(pltpu.SMEM)


def shape(*sizes, dtype=F32):
    return jax.ShapeDtypeStruct(sizes, dtype)


def run(kernel, operands, specs, outs, out_specs, scratch=(), limit=62, flops=0):
    return pl.pallas_call(
        kernel,
        out_shape=outs,
        in_specs=specs,
        out_specs=out_specs,
        scratch_shapes=list(scratch),
        compiler_params=pltpu.CompilerParams(vmem_limit_bytes=limit * MIB),
        cost_estimate=pl.CostEstimate(flops=flops, bytes_accessed=0, transcendentals=0),
    )(*operands)


def moves(pairs, sems):
    copies = [pltpu.make_async_copy(a, b, sems.at[k]) for k, (a, b) in enumerate(pairs)]
    for copy in copies:
        copy.start()
    return copies


def packed(columns, rows):
    lane = lax.broadcasted_iota(jnp.int32, (rows, LANES), 1)
    out = jnp.zeros((rows, LANES), F32)
    for k, column in enumerate(columns):
        out = jnp.where(lane == k, column, out)
    return out


def pair_of(stat, other):
    high = jnp.maximum(stat[0:1], other[0:1])
    total = high + jnp.log(jnp.exp(stat[0:1] - high) + jnp.exp(other[0:1] - high))
    share, rest = jnp.exp(stat[0:1] - total), jnp.exp(other[0:1] - total)
    return total, share * stat[1:2] + rest * other[1:2], share, rest


def turned(lines):
    rows = lines[0].shape[1]
    return jnp.concatenate(list(lines) + [jnp.zeros((LANES - len(lines), rows), F32)], axis=0).T


def first_products(where, hidden, weight, lengths):
    rows, depth = hidden.shape
    width = weight.shape[1]
    half = depth // 2
    cuts = 4
    step = depth // cuts

    def kernel(where_ref, lengths_ref, hidden_ref, weight_ref, score_ref, sent_ref, kept_ref, count_ref, left, held, score, probs, sent, kept, sems, out_sems):
        pairs = []
        for k in range(cuts):
            at = pl.ds(k * step, step)
            pairs += [(hidden_ref.at[:, at], left.at[:, at]), (weight_ref.at[at, :], held.at[at, :])]
        copies = moves(pairs, sems)
        total = lengths_ref[0]
        for k in range(1, lengths.shape[0]):
            total = total + lengths_ref[k]
        count_ref[...] = jnp.full(count_ref.shape, total.astype(F32))
        body = pl.ds(0, width)
        for k in range(cuts):
            copies[2 * k].wait()
            copies[2 * k + 1].wait()
            at = pl.ds(k * step, step)
            product = jnp.dot(left[:, at], held[at, :], preferred_element_type=F32)
            if k == 0:
                score[:, body] = product
            else:
                score[:, body] += product
        logits = score[:, body]
        top = jnp.max(logits, axis=1, keepdims=True)
        lse = top + jnp.log(jnp.sum(jnp.exp(logits - top), axis=1, keepdims=True))
        logits = logits - lse
        score[:, body] = logits
        score[:, pl.ds(width, LANES)] = packed((lse,), rows)
        probs[...] = jnp.exp(logits).astype(BF16)
        outs = [(score, score_ref), (sent, sent_ref), (kept, kept_ref)]
        copies = [pltpu.make_async_copy(*pair, out_sems.at[k]) for k, pair in enumerate(outs)]
        copies[0].start()
        core = where_ref[0]
        for k, which in ((1, 1 - core), (2, core)):
            at = pl.ds(pl.multiple_of(which * half, half), half)
            outs[k][0][...] = lax.dot_general(
                probs[...], held[at, :], ACROSS, preferred_element_type=F32
            ).astype(BF16)
            copies[k].start()
        for copy in copies:
            copy.wait()

    return run(
        kernel,
        (where, lengths, hidden, weight),
        [SMEM, SMEM, HBM, HBM],
        [shape(rows, width + LANES)] + [shape(rows, half, dtype=BF16)] * 2 + [shape(8, LANES)],
        [HBM] * 3 + [VMEM],
        [
            pltpu.VMEM((rows, depth), BF16),
            pltpu.VMEM((depth, width), BF16),
            pltpu.VMEM((rows, width + LANES), F32),
            pltpu.VMEM((rows, width), BF16),
            pltpu.VMEM((rows, half), BF16),
            pltpu.VMEM((rows, half), BF16),
            pltpu.SemaphoreType.DMA((2 * cuts,)),
            pltpu.SemaphoreType.DMA((3,)),
        ],
        flops=200 * 10**9,
    )


def middle(score, teacher, devices):
    rows, width = teacher.shape

    def kernel(score_ref, teacher_ref, grad_ref, stats_ref, block_ref, held, target, grad, lines, sems):
        copies = moves([(score_ref, held), (teacher_ref, target)], sems)
        for copy in copies:
            copy.wait()
        score = held[:, pl.ds(0, width)]
        probs = jnp.exp(score)
        advantage = score - target[...].astype(F32)
        mean = jnp.sum(probs * advantage, axis=1, keepdims=True)
        tail = held[:, pl.ds(width, LANES)]
        lse = tail[:, 0:1]
        block = packed((lse, mean + lse), rows).T[:8]
        block_ref[...] = block
        for k in range(devices):
            lines[k] = block[:2]
        stats_copy = pltpu.make_async_copy(lines, stats_ref, sems.at[2])
        stats_copy.start()
        grad[...] = (probs * (advantage - mean)).astype(BF16)
        grad_copy = pltpu.make_async_copy(grad, grad_ref, sems.at[3])
        grad_copy.start()
        stats_copy.wait()
        grad_copy.wait()

    return run(
        kernel,
        (score, teacher),
        [HBM, HBM],
        [
            shape(rows, width, dtype=BF16),
            shape(devices, 2, rows),
            shape(8, rows),
        ],
        [HBM, HBM, VMEM],
        [
            pltpu.VMEM((rows, width + LANES), F32),
            pltpu.VMEM((rows, width), BF16),
            pltpu.VMEM((rows, width), BF16),
            pltpu.VMEM((devices, 2, rows), F32),
            pltpu.SemaphoreType.DMA((4,)),
        ],
        limit=62,
        flops=50 * 10**9,
    )


def pair_products(where, blocks, lefts, weight, weight_far):
    rows, width = lefts[0].shape
    half = weight.shape[0] // 2
    cuts = 4
    step = half // cuts

    def kernel(where_ref, block_ref, block_far_ref, grad_ref, grad_far_ref, weight_ref, far_ref, slope_ref, left, held, slope, factors, sems, out_sems):
        start = pl.multiple_of(where_ref[0] * half, half)
        pairs = []
        for k in range(cuts):
            at = pl.ds(k * step, step)
            here = pl.ds(start + k * step, step)
            for j, (side, ref) in enumerate(((grad_ref, weight_ref), (grad_far_ref, far_ref))):
                if k == 0:
                    pairs.append((side, left.at[j]))
                pairs.append((ref.at[here, :], held.at[j, at, :]))
        copies = moves(pairs, sems)
        stat, other = block_ref[...], block_far_ref[...]
        _, _, share, rest = pair_of(stat, other)
        factors[...] = turned((share, rest))
        outs = []
        for k in range(cuts):
            at = pl.ds(k * step, step)
            total = None
            for j in range(2):
                for copy in copies[2 * j : 2 * j + 2] if k == 0 else copies[2 * k + 2 + j : 2 * k + 3 + j]:
                    copy.wait()
                product = factors[:, j : j + 1] * lax.dot_general(
                    left[j], held[j, at, :], ACROSS, preferred_element_type=F32
                )
                total = product if total is None else total + product
            slope[:, at] = total.astype(BF16)
            outs.append(pltpu.make_async_copy(slope.at[:, at], slope_ref.at[:, at], out_sems.at[k]))
            outs[k].start()
        for copy in outs:
            copy.wait()

    return run(
        kernel,
        (where, *blocks, *lefts, weight, weight_far),
        [SMEM, VMEM, VMEM] + [HBM] * 4,
        [shape(rows, half, dtype=BF16)],
        [HBM],
        [
            pltpu.VMEM((2, rows, width), BF16),
            pltpu.VMEM((2, half, width), BF16),
            pltpu.VMEM((rows, half), BF16),
            pltpu.VMEM((rows, LANES), F32),
            pltpu.SemaphoreType.DMA((2 + 2 * cuts,)),
            pltpu.SemaphoreType.DMA((cuts,)),
        ],
        limit=62,
        flops=200 * 10**9,
    )[0]


def merge(where, lengths, stats, products, counts, planes):
    rows, half = products[0].shape
    slot_count = rows // lengths.shape[0]
    cuts = 4
    step = half // cuts

    def kernel(where_ref, lengths_ref, stats_ref, slope_ref, base_ref, far_ref, count_ref, heard_ref, out_ref, kl_ref, both_ref, held, out, factors, sems, out_sems):
        copies = moves(
            [
                (ref.at[:, pl.ds(k * step, step)], held.at[j, :, pl.ds(k * step, step)])
                for k in range(cuts)
                for j, ref in enumerate((slope_ref, base_ref, far_ref))
            ],
            sems,
        )
        sums = stats_ref[:, 0, :]
        levels = stats_ref[:, 1, :]
        both_ref[...] = count_ref[...] + heard_ref[...]
        high = jnp.max(sums, axis=0, keepdims=True)
        share = jnp.exp(sums - high)
        whole = jnp.sum(share, axis=0, keepdims=True)
        lse = high + jnp.log(whole)
        level = jnp.sum(share * levels, axis=0, keepdims=True) / whole
        token = lax.broadcasted_iota(jnp.int32, (1, rows), 1)
        live = jnp.zeros((1, rows), F32)
        for k in range(rows // slot_count):
            inside = (token >= k * slot_count) & (token < k * slot_count + lengths_ref[k])
            live = jnp.where(inside, 1.0, live)
        start = where_ref[1] * kl_ref.shape[0]
        turn = lax.rem(rows - start, rows)
        kl = jnp.broadcast_to(live * (level - lse), (8, rows))
        kl_ref[...] = pltpu.roll(kl, turn, 1)[0, : kl_ref.shape[0]]
        own, other = (stats_ref[where_ref[k]] for k in (1, 2))
        total, _, near, far = pair_of(own, other)
        factor = live * jnp.exp(total - lse)
        factors[...] = turned(
            (factor, factor * near * (own[1:2] - level), factor * far * (other[1:2] - level))
        )
        outs = []
        for k in range(cuts):
            at = pl.ds(k * step, step)
            value = None
            for j in range(3):
                copies[3 * k + j].wait()
                term = factors[:, j : j + 1] * held[j, :, at].astype(F32)
                value = term if value is None else value + term
            group = rows // stats.shape[0] * 2
            value = value.reshape(rows // (group * planes), planes, group, step)
            for z in range(planes):
                each = rows // planes
                out[pl.ds(z * each, each), at] = value[:, z].reshape(each, step).astype(BF16)
            outs.append(pltpu.make_async_copy(out.at[:, at], out_ref.at[:, at], out_sems.at[k]))
            outs[k].start()
        for copy in outs:
            copy.wait()

    return run(
        kernel,
        (where, lengths, stats, *products, *counts),
        [SMEM, SMEM, VMEM] + [HBM] * 3 + [VMEM] * 2,
        [shape(rows, half, dtype=BF16), shape(rows // stats.shape[0]), shape(8, LANES)],
        [HBM, VMEM, VMEM],
        [
            pltpu.VMEM((3, rows, half), BF16),
            pltpu.VMEM((rows, half), BF16),
            pltpu.VMEM((rows, LANES), F32),
            pltpu.SemaphoreType.DMA((3 * cuts,)),
            pltpu.SemaphoreType.DMA((cuts,)),
        ],
    )


def shares(where, counts, spread, own_rows, scale):
    half = spread.shape[2]

    def kernel(where_ref, spread_ref, *refs):
        keep_ref, give_ref = refs[len(counts) :]
        count = sum(ref[0:1, 0:1] for ref in refs[: len(counts)])
        total = jnp.sum(spread_ref[...].astype(F32), axis=0) * (scale / count)
        first, second = total[:own_rows], total[own_rows:]
        own = where_ref[0] == 0
        keep_ref[...] = jnp.where(own, first, second)
        give_ref[...] = jnp.where(own, second, first)

    return run(
        kernel,
        (where, spread, *counts),
        [SMEM, VMEM] + [VMEM] * len(counts),
        [shape(own_rows, half)] * 2,
        [VMEM] * 2,
        limit=16,
    )


def joined(where, keep, get):
    own_rows, half = keep.shape

    def kernel(where_ref, keep_ref, get_ref, out_ref):
        own = where_ref[0] == 0
        keep, get = keep_ref[...], get_ref[...]
        out_ref[:, :half] = jnp.where(own, keep, get).astype(BF16)
        out_ref[:, half:] = jnp.where(own, get, keep).astype(BF16)

    return run(
        kernel,
        (where, keep, get),
        [SMEM, VMEM, VMEM],
        [shape(own_rows, 2 * half, dtype=BF16)],
        [VMEM],
        limit=16,
    )[0]


def body(student_hidden, head_weight, teacher_logprob, lengths):
    rows, depth = student_hidden.shape
    devices = lax.axis_size(VOCAB)
    own_rows = rows // devices
    seq_devices = lax.axis_size("seq")
    core = lax.axis_index("core").astype(jnp.int32)
    place = lax.axis_index(VOCAB).astype(jnp.int32)
    where = jnp.stack([core, place, place + 1 - 2 * core])

    def swap(value):
        return lax.ppermute(value, "core", [(0, 1), (1, 0)])

    def across(value, bit):
        return lax.ppermute(value, "seq", [(s, s ^ bit) for s in range(seq_devices)])

    def whole(value, axes):
        return lax.all_to_all(value, axes, split_axis=0, concat_axis=0, tiled=True)

    teacher = lax.all_to_all(teacher_logprob, VOCAB, split_axis=1, concat_axis=0, tiled=True)
    weight_far = swap(head_weight)
    score, base_sent, base, count = first_products(where, student_hidden, head_weight, lengths)
    base_far = swap(base_sent)
    counts = (count, across(count, 1))

    grad, stats, block = middle(score, teacher, devices)
    grad_far = swap(grad)
    block_far = swap(block)
    stats = whole(stats, VOCAB)
    slope = pair_products(where, (block, block_far), (grad, grad_far), head_weight, weight_far)

    chip_sum, token_kl, count = merge(
        where, lengths, stats, (slope, base, base_far), counts, lax.axis_size("z")
    )
    spread = whole(chip_sum.reshape(devices // 2, 2 * own_rows, depth // 2), ("z", "y", "x"))
    counts = [count] + [across(count, bit) for bit in range(2, seq_devices, 2)]
    keep, give = shares(where, counts, spread, own_rows, float(rows * seq_devices))
    hidden_grad = joined(where, keep, swap(give))
    return hidden_grad, token_kl


def solution(mesh, sizes=(4, 4, 4, 2, 2)):
    return jax.shard_map(
        body,
        mesh=Mesh(mesh.devices.reshape(sizes), ALL),
        in_specs=(P("seq", None), P(None, VOCAB), P(ALL, None), P("seq")),
        out_specs=(P(ALL, None), P(ALL)),
        check_vma=False,
    )
```

```python
import jax
import jax.numpy as jnp
from jax import lax
from jax.experimental import pallas as pl
from jax.experimental.pallas import tpu as pltpu
from jax.sharding import Mesh, PartitionSpec as P

VOCAB = ("y", "x", "z", "core")
ALL = ("seq",) + VOCAB
F32 = jnp.float32
BF16 = jnp.bfloat16
MIB = 2**20
LANES = 128
ACROSS = (((1,), (1,)), ((), ()))


def place_of(memory):
    return pl.BlockSpec(memory_space=memory)


VMEM = place_of(pltpu.VMEM)
HBM = place_of(pltpu.HBM)
SMEM = place_of(pltpu.SMEM)


def shape(*sizes, dtype=F32):
    return jax.ShapeDtypeStruct(sizes, dtype)


def run(kernel, operands, specs, outs, out_specs, scratch=(), limit=62, flops=0):
    return pl.pallas_call(
        kernel,
        out_shape=outs,
        in_specs=specs,
        out_specs=out_specs,
        scratch_shapes=list(scratch),
        compiler_params=pltpu.CompilerParams(vmem_limit_bytes=limit * MIB),
        cost_estimate=pl.CostEstimate(flops=flops, bytes_accessed=0, transcendentals=0),
    )(*operands)


def moves(pairs, sems):
    copies = [pltpu.make_async_copy(a, b, sems.at[k]) for k, (a, b) in enumerate(pairs)]
    for copy in copies:
        copy.start()
    return copies


def packed(columns, rows):
    lane = lax.broadcasted_iota(jnp.int32, (rows, LANES), 1)
    out = jnp.zeros((rows, LANES), F32)
    for k, column in enumerate(columns):
        out = jnp.where(lane == k, column, out)
    return out


def turned(lines):
    rows = lines[0].shape[1]
    return jnp.concatenate(list(lines) + [jnp.zeros((LANES - len(lines), rows), F32)], axis=0).T


def first_products(where, hidden, weight, lengths):
    rows, depth = hidden.shape
    width = weight.shape[1]
    half = depth // 2
    cuts = 4
    step = depth // cuts

    def kernel(where_ref, lengths_ref, hidden_ref, weight_ref, score_ref, probs_ref, base_ref, count_ref, left, held, score, probs, base, sems, out_sems):
        pairs = []
        for k in range(cuts):
            at = pl.ds(k * step, step)
            pairs += [(hidden_ref.at[:, at], left.at[:, at]), (weight_ref.at[at, :], held.at[at, :])]
        copies = moves(pairs, sems)
        total = lengths_ref[0]
        for k in range(1, lengths.shape[0]):
            total = total + lengths_ref[k]
        count_ref[...] = jnp.full(count_ref.shape, total.astype(F32))
        body = pl.ds(0, width)
        for k in range(cuts):
            copies[2 * k].wait()
            copies[2 * k + 1].wait()
            at = pl.ds(k * step, step)
            product = jnp.dot(left[:, at], held[at, :], preferred_element_type=F32)
            if k == 0:
                score[:, body] = product
            else:
                score[:, body] += product
        logits = score[:, body]
        top = jnp.max(logits, axis=1, keepdims=True)
        mass = jnp.exp(logits - top)
        total = jnp.sum(mass, axis=1, keepdims=True)
        probs[...] = (mass * (1.0 / total)).astype(BF16)
        outs = [(probs, probs_ref), (score, score_ref), (base, base_ref)]
        copies = [pltpu.make_async_copy(*pair, out_sems.at[k]) for k, pair in enumerate(outs)]
        copies[0].start()
        lse = top + jnp.log(total)
        score[:, body] = logits - lse
        score[:, pl.ds(width, LANES)] = packed((lse,), rows)
        copies[1].start()
        at = pl.ds(pl.multiple_of(where_ref[0] * half, half), half)
        base[...] = lax.dot_general(
            probs[...], held[at, :], ACROSS, preferred_element_type=F32
        ).astype(BF16)
        copies[2].start()
        for copy in copies:
            copy.wait()

    return run(
        kernel,
        (where, lengths, hidden, weight),
        [SMEM, SMEM, HBM, HBM],
        [
            shape(rows, width + LANES),
            shape(rows, width, dtype=BF16),
            shape(rows, half, dtype=BF16),
            shape(8, LANES),
        ],
        [HBM] * 3 + [VMEM],
        [
            pltpu.VMEM((rows, depth), BF16),
            pltpu.VMEM((depth, width), BF16),
            pltpu.VMEM((rows, width + LANES), F32),
            pltpu.VMEM((rows, width), BF16),
            pltpu.VMEM((rows, half), BF16),
            pltpu.SemaphoreType.DMA((2 * cuts,)),
            pltpu.SemaphoreType.DMA((3,)),
        ],
        flops=200 * 10**9,
    )


def near_product(where, left, weight):
    rows, width = left.shape
    half = weight.shape[0] // 2
    cuts = 4
    step = half // cuts

    def kernel(where_ref, left_ref, weight_ref, out_ref, side, held, out, sems, out_sems):
        start = pl.multiple_of(where_ref[0] * half, half)
        pairs = [(left_ref, side)]
        for k in range(cuts):
            pairs.append((weight_ref.at[pl.ds(start + k * step, step), :], held.at[pl.ds(k * step, step), :]))
        copies = moves(pairs, sems)
        copies[0].wait()
        outs = []
        for k in range(cuts):
            at = pl.ds(k * step, step)
            copies[1 + k].wait()
            out[:, at] = lax.dot_general(
                side[...], held[at, :], ACROSS, preferred_element_type=F32
            ).astype(BF16)
            outs.append(pltpu.make_async_copy(out.at[:, at], out_ref.at[:, at], out_sems.at[k]))
            outs[k].start()
        for copy in outs:
            copy.wait()

    return run(
        kernel,
        (where, left, weight),
        [SMEM, HBM, HBM],
        [shape(rows, half, dtype=BF16)],
        [HBM],
        [
            pltpu.VMEM((rows, width), BF16),
            pltpu.VMEM((half, width), BF16),
            pltpu.VMEM((rows, half), BF16),
            pltpu.SemaphoreType.DMA((1 + cuts,)),
            pltpu.SemaphoreType.DMA((cuts,)),
        ],
        flops=50 * 10**9,
    )[0]


def middle(score, teacher, devices):
    rows, width = teacher.shape

    def kernel(score_ref, teacher_ref, grad_ref, stats_ref, held, target, grad, lines, sems):
        copies = moves([(score_ref, held), (teacher_ref, target)], sems)
        for copy in copies:
            copy.wait()
        score = held[:, pl.ds(0, width)]
        probs = jnp.exp(score)
        advantage = score - target[...].astype(F32)
        mean = jnp.sum(probs * advantage, axis=1, keepdims=True)
        lse = held[:, pl.ds(width, LANES)][:, 0:1]
        block = packed((lse, mean + lse), rows).T[:2]
        for k in range(devices):
            lines[k] = block
        stats_copy = pltpu.make_async_copy(lines, stats_ref, sems.at[2])
        stats_copy.start()
        grad[...] = (probs * (advantage - mean)).astype(BF16)
        grad_copy = pltpu.make_async_copy(grad, grad_ref, sems.at[3])
        grad_copy.start()
        stats_copy.wait()
        grad_copy.wait()

    return run(
        kernel,
        (score, teacher),
        [HBM, HBM],
        [shape(rows, width, dtype=BF16), shape(devices, 2, rows)],
        [HBM, HBM],
        [
            pltpu.VMEM((rows, width + LANES), F32),
            pltpu.VMEM((rows, width), BF16),
            pltpu.VMEM((rows, width), BF16),
            pltpu.VMEM((devices, 2, rows), F32),
            pltpu.SemaphoreType.DMA((4,)),
        ],
        flops=50 * 10**9,
    )


def chip_products(where, lengths, stats, lefts, weight_far, products, counts, planes):
    rows, half = products[0].shape
    width = weight_far.shape[1]
    slot_count = rows // lengths.shape[0]
    cuts = 4
    step = half // cuts

    def kernel(where_ref, lengths_ref, stats_ref, grad_ref, probs_ref, far_ref, near_ref, base_ref, count_ref, out_ref, kl_ref, passed_ref, left, side, held, mine, out, factors, sems, out_sems):
        start = pl.multiple_of(where_ref[0] * half, half)
        pairs = [(grad_ref, left.at[0]), (probs_ref, left.at[1])]
        for k in range(cuts):
            at = pl.ds(k * step, step)
            pairs += [
                (far_ref.at[pl.ds(start + k * step, step), :], held.at[at, :]),
                (near_ref.at[:, at], mine.at[0, :, at]),
                (base_ref.at[:, at], mine.at[1, :, at]),
            ]
        copies = moves(pairs, sems)
        passed_ref[...] = count_ref[...]
        sums = stats_ref[:, 0, :]
        levels = stats_ref[:, 1, :]
        high = jnp.max(sums, axis=0, keepdims=True)
        share = jnp.exp(sums - high)
        whole = jnp.sum(share, axis=0, keepdims=True)
        lse = high + jnp.log(whole)
        level = jnp.sum(share * levels, axis=0, keepdims=True) / whole
        token = lax.broadcasted_iota(jnp.int32, (1, rows), 1)
        live = jnp.zeros((1, rows), F32)
        for k in range(rows // slot_count):
            inside = (token >= k * slot_count) & (token < k * slot_count + lengths_ref[k])
            live = jnp.where(inside, 1.0, live)
        own_rows = kl_ref.shape[0]
        turn = lax.rem(rows - where_ref[1] * own_rows, rows)
        kl = jnp.broadcast_to(live * (level - lse), (8, rows))
        kl_ref[...] = pltpu.roll(kl, turn, 1)[0, :own_rows]
        lines = []
        for k in (1, 2):
            stat = stats_ref[where_ref[k]]
            factor = live * jnp.exp(stat[0:1] - lse)
            lines += [factor, factor * (stat[1:2] - level)]
        factors[...] = turned(lines)
        copies[0].wait()
        copies[1].wait()
        side[...] = (
            factors[:, 2:3] * left[0].astype(F32) + factors[:, 3:4] * left[1].astype(F32)
        ).astype(BF16)
        outs = []
        group = rows // stats.shape[0] * 2
        each = rows // planes
        for k in range(cuts):
            at = pl.ds(k * step, step)
            for j in range(3):
                copies[2 + 3 * k + j].wait()
            value = lax.dot_general(side[...], held[at, :], ACROSS, preferred_element_type=F32)
            for j in range(2):
                value = value + factors[:, j : j + 1] * mine[j, :, at].astype(F32)
            value = value.reshape(rows // (group * planes), planes, group, step)
            for z in range(planes):
                out[pl.ds(z * each, each), at] = value[:, z].reshape(each, step).astype(BF16)
            outs.append(pltpu.make_async_copy(out.at[:, at], out_ref.at[:, at], out_sems.at[k]))
            outs[k].start()
        for copy in outs:
            copy.wait()

    return run(
        kernel,
        (where, lengths, stats, *lefts, weight_far, *products, *counts),
        [SMEM, SMEM, VMEM] + [HBM] * 5 + [VMEM],
        [shape(rows, half, dtype=BF16), shape(rows // stats.shape[0]), shape(8, LANES)],
        [HBM, VMEM, VMEM],
        [
            pltpu.VMEM((2, rows, width), BF16),
            pltpu.VMEM((rows, width), BF16),
            pltpu.VMEM((half, width), BF16),
            pltpu.VMEM((2, rows, half), BF16),
            pltpu.VMEM((rows, half), BF16),
            pltpu.VMEM((rows, LANES), F32),
            pltpu.SemaphoreType.DMA((2 + 3 * cuts,)),
            pltpu.SemaphoreType.DMA((cuts,)),
        ],
    )


def body(student_hidden, head_weight, teacher_logprob, lengths):
    rows, depth = student_hidden.shape
    devices = lax.axis_size(VOCAB)
    own_rows = rows // devices
    seq_devices = lax.axis_size("seq")
    core = lax.axis_index("core").astype(jnp.int32)
    place = lax.axis_index(VOCAB).astype(jnp.int32)
    where = jnp.stack([core, place, place + 1 - 2 * core])

    def swap(value):
        return lax.ppermute(value, "core", [(0, 1), (1, 0)])

    def across(value, step):
        return lax.ppermute(value, "seq", [(s, (s + step) % seq_devices) for s in range(seq_devices)])

    def whole(value, axes):
        return lax.all_to_all(value, axes, split_axis=0, concat_axis=0, tiled=True)

    teacher = lax.all_to_all(teacher_logprob, VOCAB, split_axis=1, concat_axis=0, tiled=True)
    weight_far = swap(head_weight)
    score, probs, base, count = first_products(where, student_hidden, head_weight, lengths)
    probs_far = swap(probs)

    grad, stats = middle(score, teacher, devices)
    grad_far = swap(grad)
    stats = whole(stats, VOCAB)
    near = near_product(where, grad, head_weight)

    chip_sum, token_kl, count = chip_products(
        where,
        lengths,
        stats,
        (grad_far, probs_far),
        weight_far,
        (near, base),
        (count,),
        lax.axis_size("z"),
    )
    spread = whole(chip_sum.reshape(devices // 2, 2 * own_rows, depth // 2), ("z", "y", "x"))
    count = count + sum(across(count, step) for step in range(1, seq_devices))
    summed = jnp.sum(spread.astype(F32), axis=0) * (float(rows * seq_devices) / count[0, 0])
    first, second = summed[:own_rows], summed[own_rows:]
    own = core == 0
    keep = jnp.where(own, first, second).astype(BF16)
    get = swap(jnp.where(own, second, first).astype(BF16))
    hidden_grad = jnp.concatenate([jnp.where(own, keep, get), jnp.where(own, get, keep)], axis=1)
    return hidden_grad, token_kl


def solution(mesh, sizes=(4, 4, 4, 2, 2)):
    return jax.shard_map(
        body,
        mesh=Mesh(mesh.devices.reshape(sizes), ALL),
        in_specs=(P("seq", None), P(None, VOCAB), P(ALL, None), P("seq")),
        out_specs=(P(ALL, None), P(ALL)),
        check_vma=False,
    )
```

```python
import jax
import jax.numpy as jnp
from jax import lax
from jax.experimental import pallas as pl
from jax.experimental.pallas import tpu as pltpu
from jax.sharding import Mesh, PartitionSpec as P

VOCAB = ("y", "x", "z", "core")
ALL = ("seq",) + VOCAB
F32 = jnp.float32
BF16 = jnp.bfloat16
MIB = 2**20
LANES = 128
ACROSS = (((1,), (1,)), ((), ()))


def place_of(memory):
    return pl.BlockSpec(memory_space=memory)


VMEM = place_of(pltpu.VMEM)
HBM = place_of(pltpu.HBM)
SMEM = place_of(pltpu.SMEM)


def shape(*sizes, dtype=F32):
    return jax.ShapeDtypeStruct(sizes, dtype)


def run(kernel, operands, specs, outs, out_specs, scratch=(), limit=62, flops=0):
    return pl.pallas_call(
        kernel,
        out_shape=outs,
        in_specs=specs,
        out_specs=out_specs,
        scratch_shapes=list(scratch),
        compiler_params=pltpu.CompilerParams(vmem_limit_bytes=limit * MIB),
        cost_estimate=pl.CostEstimate(flops=flops, bytes_accessed=0, transcendentals=0),
    )(*operands)


def moves(pairs, sems):
    copies = [pltpu.make_async_copy(a, b, sems.at[k]) for k, (a, b) in enumerate(pairs)]
    for copy in copies:
        copy.start()
    return copies


def packed(columns, rows):
    lane = lax.broadcasted_iota(jnp.int32, (rows, LANES), 1)
    out = jnp.zeros((rows, LANES), F32)
    for k, column in enumerate(columns):
        out = jnp.where(lane == k, column, out)
    return out


def turned(lines):
    rows = lines[0].shape[1]
    return jnp.concatenate(list(lines) + [jnp.zeros((LANES - len(lines), rows), F32)], axis=0).T


def first_products(where, hidden, weight, lengths):
    rows, depth = hidden.shape
    width = weight.shape[1]
    half = depth // 2
    cuts = 4
    step = depth // cuts

    def kernel(where_ref, lengths_ref, hidden_ref, weight_ref, score_ref, probs_ref, base_ref, count_ref, left, held, score, probs, base, sems, out_sems):
        pairs = []
        for k in range(cuts):
            at = pl.ds(k * step, step)
            pairs += [(hidden_ref.at[:, at], left.at[:, at]), (weight_ref.at[at, :], held.at[at, :])]
        copies = moves(pairs, sems)
        total = lengths_ref[0]
        for k in range(1, lengths.shape[0]):
            total = total + lengths_ref[k]
        count_ref[...] = jnp.full(count_ref.shape, total.astype(F32))
        body = pl.ds(0, width)
        for k in range(cuts):
            copies[2 * k].wait()
            copies[2 * k + 1].wait()
            at = pl.ds(k * step, step)
            product = jnp.dot(left[:, at], held[at, :], preferred_element_type=F32)
            if k == 0:
                score[:, body] = product
            else:
                score[:, body] += product
        logits = score[:, body]
        top = jnp.max(logits, axis=1, keepdims=True)
        mass = jnp.exp(logits - top)
        total = jnp.sum(mass, axis=1, keepdims=True)
        probs[...] = (mass * (1.0 / total)).astype(BF16)
        outs = [(probs, probs_ref), (score, score_ref), (base, base_ref)]
        copies = [pltpu.make_async_copy(*pair, out_sems.at[k]) for k, pair in enumerate(outs)]
        copies[0].start()
        lse = top + jnp.log(total)
        score[:, body] = logits - lse
        score[:, pl.ds(width, LANES)] = packed((lse,), rows)
        copies[1].start()
        at = pl.ds(pl.multiple_of(where_ref[0] * half, half), half)
        base[...] = lax.dot_general(
            probs[...], held[at, :], ACROSS, preferred_element_type=F32
        ).astype(BF16)
        copies[2].start()
        for copy in copies:
            copy.wait()

    return run(
        kernel,
        (where, lengths, hidden, weight),
        [SMEM, SMEM, HBM, HBM],
        [
            shape(rows, width + LANES),
            shape(rows, width, dtype=BF16),
            shape(rows, half, dtype=BF16),
            shape(8, LANES),
        ],
        [HBM] * 3 + [VMEM],
        [
            pltpu.VMEM((rows, depth), BF16),
            pltpu.VMEM((depth, width), BF16),
            pltpu.VMEM((rows, width + LANES), F32),
            pltpu.VMEM((rows, width), BF16),
            pltpu.VMEM((rows, half), BF16),
            pltpu.SemaphoreType.DMA((2 * cuts,)),
            pltpu.SemaphoreType.DMA((3,)),
        ],
        flops=200 * 10**9,
    )


def near_product(where, left, weight):
    rows, width = left.shape
    half = weight.shape[0] // 2
    cuts = 4
    step = half // cuts

    def kernel(where_ref, left_ref, weight_ref, out_ref, side, held, out, sems, out_sems):
        start = pl.multiple_of(where_ref[0] * half, half)
        pairs = [(left_ref, side)]
        for k in range(cuts):
            pairs.append((weight_ref.at[pl.ds(start + k * step, step), :], held.at[pl.ds(k * step, step), :]))
        copies = moves(pairs, sems)
        copies[0].wait()
        outs = []
        for k in range(cuts):
            at = pl.ds(k * step, step)
            copies[1 + k].wait()
            out[:, at] = lax.dot_general(
                side[...], held[at, :], ACROSS, preferred_element_type=F32
            ).astype(BF16)
            outs.append(pltpu.make_async_copy(out.at[:, at], out_ref.at[:, at], out_sems.at[k]))
            outs[k].start()
        for copy in outs:
            copy.wait()

    return run(
        kernel,
        (where, left, weight),
        [SMEM, HBM, HBM],
        [shape(rows, half, dtype=BF16)],
        [HBM],
        [
            pltpu.VMEM((rows, width), BF16),
            pltpu.VMEM((half, width), BF16),
            pltpu.VMEM((rows, half), BF16),
            pltpu.SemaphoreType.DMA((1 + cuts,)),
            pltpu.SemaphoreType.DMA((cuts,)),
        ],
        flops=50 * 10**9,
    )[0]


def middle(score, teacher, devices):
    rows, width = teacher.shape

    def kernel(score_ref, teacher_ref, grad_ref, stats_ref, held, target, grad, lines, sems):
        copies = moves([(score_ref, held), (teacher_ref, target)], sems)
        for copy in copies:
            copy.wait()
        score = held[:, pl.ds(0, width)]
        probs = jnp.exp(score)
        advantage = score - target[...].astype(F32)
        mean = jnp.sum(probs * advantage, axis=1, keepdims=True)
        lse = held[:, pl.ds(width, LANES)][:, 0:1]
        block = packed((lse, mean + lse), rows).T[:2]
        for k in range(devices):
            lines[k] = block
        stats_copy = pltpu.make_async_copy(lines, stats_ref, sems.at[2])
        stats_copy.start()
        grad[...] = (probs * (advantage - mean)).astype(BF16)
        grad_copy = pltpu.make_async_copy(grad, grad_ref, sems.at[3])
        grad_copy.start()
        stats_copy.wait()
        grad_copy.wait()

    return run(
        kernel,
        (score, teacher),
        [HBM, HBM],
        [shape(rows, width, dtype=BF16), shape(devices, 2, rows)],
        [HBM, HBM],
        [
            pltpu.VMEM((rows, width + LANES), F32),
            pltpu.VMEM((rows, width), BF16),
            pltpu.VMEM((rows, width), BF16),
            pltpu.VMEM((devices, 2, rows), F32),
            pltpu.SemaphoreType.DMA((4,)),
        ],
        flops=50 * 10**9,
    )


def chip_products(where, lengths, stats, lefts, weight_far, products, counts, sizes):
    ny, nx, nz = sizes
    rows, half = products[0].shape
    width = weight_far.shape[1]
    slot_count = rows // lengths.shape[0]
    cuts = 4
    step = half // cuts

    def kernel(where_ref, lengths_ref, stats_ref, grad_ref, probs_ref, far_ref, near_ref, base_ref, count_ref, out_ref, kl_ref, passed_ref, left, side, held, mine, out, factors, sems, out_sems):
        start = pl.multiple_of(where_ref[0] * half, half)
        pairs = [(grad_ref, left)]
        for k in range(cuts):
            at = pl.ds(k * step, step)
            pairs += [
                (far_ref.at[pl.ds(start + k * step, step), :], held.at[at, :]),
                (near_ref.at[:, at], mine.at[0, :, at]),
                (base_ref.at[:, at], mine.at[1, :, at]),
            ]
        copies = moves(pairs, sems)
        passed_ref[...] = count_ref[...]
        sums = stats_ref[:, 0, :]
        levels = stats_ref[:, 1, :]
        high = jnp.max(sums, axis=0, keepdims=True)
        share = jnp.exp(sums - high)
        whole = jnp.sum(share, axis=0, keepdims=True)
        lse = high + jnp.log(whole)
        level = jnp.sum(share * levels, axis=0, keepdims=True) / whole
        token = lax.broadcasted_iota(jnp.int32, (1, rows), 1)
        live = jnp.zeros((1, rows), F32)
        for k in range(rows // slot_count):
            inside = (token >= k * slot_count) & (token < k * slot_count + lengths_ref[k])
            live = jnp.where(inside, 1.0, live)
        own_rows = kl_ref.shape[0]
        turn = lax.rem(rows - where_ref[1] * own_rows, rows)
        kl = jnp.broadcast_to(live * (level - lse), (8, rows))
        kl_ref[...] = pltpu.roll(kl, turn, 1)[0, :own_rows]
        lines = []
        for k in (1, 2):
            stat = stats_ref[where_ref[k]]
            factor = live * jnp.exp(stat[0:1] - lse)
            lines += [factor, factor * (stat[1:2] - level)]
        factors[...] = turned(lines)
        copies[0].wait()
        side[...] = (
            factors[:, 2:3] * left[...].astype(F32) + factors[:, 3:4] * probs_ref[...].astype(F32)
        ).astype(BF16)
        outs = []
        for k in range(cuts):
            at = pl.ds(k * step, step)
            for j in range(3):
                copies[1 + 3 * k + j].wait()
            value = lax.dot_general(side[...], held[at, :], ACROSS, preferred_element_type=F32)
            for j in range(2):
                value = value + factors[:, j : j + 1] * mine[j, :, at].astype(F32)
            value = value.reshape(ny, nx * nz * 2, own_rows, step)
            each = ny * own_rows
            for x in range(nx):
                for z in range(nz):
                    for c in range(2):
                        spot = (c * nz + z) * nx + x
                        out[pl.ds(spot * each, each), at] = (
                            value[:, (x * nz + z) * 2 + c].reshape(each, step).astype(BF16)
                        )
            outs.append(pltpu.make_async_copy(out.at[:, at], out_ref.at[:, at], out_sems.at[k]))
            outs[k].start()
        for copy in outs:
            copy.wait()

    return run(
        kernel,
        (where, lengths, stats, *lefts, weight_far, *products, *counts),
        [SMEM, SMEM, VMEM, HBM, VMEM] + [HBM] * 3 + [VMEM],
        [shape(rows, half, dtype=BF16), shape(rows // stats.shape[0]), shape(8, LANES)],
        [HBM, VMEM, VMEM],
        [
            pltpu.VMEM((rows, width), BF16),
            pltpu.VMEM((rows, width), BF16),
            pltpu.VMEM((half, width), BF16),
            pltpu.VMEM((2, rows, half), BF16),
            pltpu.VMEM((rows, half), BF16),
            pltpu.VMEM((rows, LANES), F32),
            pltpu.SemaphoreType.DMA((1 + 3 * cuts,)),
            pltpu.SemaphoreType.DMA((cuts,)),
        ],
        limit=48,
    )


def body(student_hidden, head_weight, teacher_logprob, lengths):
    rows, depth = student_hidden.shape
    devices = lax.axis_size(VOCAB)
    own_rows = rows // devices
    seq_devices = lax.axis_size("seq")
    core = lax.axis_index("core").astype(jnp.int32)
    place = lax.axis_index(VOCAB).astype(jnp.int32)
    where = jnp.stack([core, place, place + 1 - 2 * core])

    def swap(value):
        return lax.ppermute(value, "core", [(0, 1), (1, 0)])

    def across(value, step):
        return lax.ppermute(value, "seq", [(s, (s + step) % seq_devices) for s in range(seq_devices)])

    def whole(value, axes):
        return lax.all_to_all(value, axes, split_axis=0, concat_axis=0, tiled=True)

    teacher = lax.all_to_all(teacher_logprob, VOCAB, split_axis=1, concat_axis=0, tiled=True)
    weight_far = swap(head_weight)
    score, probs, base, count = first_products(where, student_hidden, head_weight, lengths)
    probs_far = swap(probs)

    grad, stats = middle(score, teacher, devices)
    grad_far = swap(grad)
    stats = whole(stats, VOCAB)
    near = near_product(where, grad, head_weight)

    chip_sum, token_kl, count = chip_products(
        where,
        lengths,
        stats,
        (grad_far, probs_far),
        weight_far,
        (near, base),
        (count,),
        tuple(lax.axis_size(axis) for axis in ("y", "x", "z")),
    )
    spread = whole(
        chip_sum.reshape(devices, own_rows, depth // 2), ("core", "z", "x", "y")
    )
    count = count + sum(across(count, step) for step in range(1, seq_devices))
    summed = jnp.sum(spread.astype(F32).reshape(2, devices // 2, own_rows, depth // 2), axis=1)
    rounded = (summed * (float(rows * seq_devices) / count[0, 0])).astype(BF16)
    hidden_grad = jnp.concatenate([rounded[0], rounded[1]], axis=1)
    return hidden_grad, token_kl


def solution(mesh, sizes=(4, 4, 4, 2, 2)):
    return jax.shard_map(
        body,
        mesh=Mesh(mesh.devices.reshape(sizes), ALL),
        in_specs=(P("seq", None), P(None, VOCAB), P(ALL, None), P("seq")),
        out_specs=(P(ALL, None), P(ALL)),
        check_vma=False,
    )
```

```python
import jax
import jax.numpy as jnp
from jax import lax
from jax.experimental import pallas as pl
from jax.experimental.pallas import tpu as pltpu
from jax.sharding import Mesh, PartitionSpec as P

VOCAB = ("y", "x", "z", "core")
ALL = ("seq",) + VOCAB
F32 = jnp.float32
BF16 = jnp.bfloat16
MIB = 2**20
LANES = 128
ACROSS = (((1,), (1,)), ((), ()))


def place_of(memory):
    return pl.BlockSpec(memory_space=memory)


VMEM = place_of(pltpu.VMEM)
HBM = place_of(pltpu.HBM)
SMEM = place_of(pltpu.SMEM)


def shape(*sizes, dtype=F32):
    return jax.ShapeDtypeStruct(sizes, dtype)


def run(kernel, operands, specs, outs, out_specs, scratch=(), limit=62, flops=0):
    return pl.pallas_call(
        kernel,
        out_shape=outs,
        in_specs=specs,
        out_specs=out_specs,
        scratch_shapes=list(scratch),
        compiler_params=pltpu.CompilerParams(vmem_limit_bytes=limit * MIB),
        cost_estimate=pl.CostEstimate(flops=flops, bytes_accessed=0, transcendentals=0),
    )(*operands)


def moves(pairs, sems):
    copies = [pltpu.make_async_copy(a, b, sems.at[k]) for k, (a, b) in enumerate(pairs)]
    for copy in copies:
        copy.start()
    return copies


def packed(columns, rows):
    lane = lax.broadcasted_iota(jnp.int32, (rows, LANES), 1)
    out = jnp.zeros((rows, LANES), F32)
    for k, column in enumerate(columns):
        out = jnp.where(lane == k, column, out)
    return out


def turned(lines):
    rows = lines[0].shape[1]
    return jnp.concatenate(list(lines) + [jnp.zeros((LANES - len(lines), rows), F32)], axis=0).T


def first_products(where, hidden, weight, lengths):
    rows, depth = hidden.shape
    width = weight.shape[1]
    half = depth // 2
    cuts = 4
    step = depth // cuts

    def kernel(where_ref, lengths_ref, hidden_ref, weight_ref, score_ref, probs_ref, base_ref, count_ref, left, held, score, probs, base, sems, out_sems):
        pairs = []
        for k in range(cuts):
            at = pl.ds(k * step, step)
            pairs += [(hidden_ref.at[:, at], left.at[:, at]), (weight_ref.at[at, :], held.at[at, :])]
        copies = moves(pairs, sems)
        total = lengths_ref[0]
        for k in range(1, lengths.shape[0]):
            total = total + lengths_ref[k]
        count_ref[...] = jnp.full(count_ref.shape, total.astype(F32))
        body = pl.ds(0, width)
        for k in range(cuts):
            copies[2 * k].wait()
            copies[2 * k + 1].wait()
            at = pl.ds(k * step, step)
            product = jnp.dot(left[:, at], held[at, :], preferred_element_type=F32)
            if k == 0:
                score[:, body] = product
            else:
                score[:, body] += product
        logits = score[:, body]
        top = jnp.max(logits, axis=1, keepdims=True)
        mass = jnp.exp(logits - top)
        total = jnp.sum(mass, axis=1, keepdims=True)
        probs[...] = (mass * (1.0 / total)).astype(BF16)
        outs = [(probs, probs_ref), (score, score_ref), (base, base_ref)]
        copies = [pltpu.make_async_copy(*pair, out_sems.at[k]) for k, pair in enumerate(outs)]
        copies[0].start()
        lse = top + jnp.log(total)
        score[:, body] = logits - lse
        score[:, pl.ds(width, LANES)] = packed((lse,), rows)
        copies[1].start()
        at = pl.ds(pl.multiple_of(where_ref[0] * half, half), half)
        base[...] = lax.dot_general(
            probs[...], held[at, :], ACROSS, preferred_element_type=F32
        ).astype(BF16)
        copies[2].start()
        for copy in copies:
            copy.wait()

    return run(
        kernel,
        (where, lengths, hidden, weight),
        [SMEM, SMEM, HBM, HBM],
        [
            shape(rows, width + LANES),
            shape(rows, width, dtype=BF16),
            shape(rows, half, dtype=BF16),
            shape(8, LANES),
        ],
        [HBM] * 3 + [VMEM],
        [
            pltpu.VMEM((rows, depth), BF16),
            pltpu.VMEM((depth, width), BF16),
            pltpu.VMEM((rows, width + LANES), F32),
            pltpu.VMEM((rows, width), BF16),
            pltpu.VMEM((rows, half), BF16),
            pltpu.SemaphoreType.DMA((2 * cuts,)),
            pltpu.SemaphoreType.DMA((3,)),
        ],
        flops=200 * 10**9,
    )


def near_product(where, left, weight):
    rows, width = left.shape
    half = weight.shape[0] // 2
    cuts = 4
    step = half // cuts

    def kernel(where_ref, left_ref, weight_ref, out_ref, side, held, out, sems, out_sems):
        start = pl.multiple_of(where_ref[0] * half, half)
        pairs = [(left_ref, side)]
        for k in range(cuts):
            pairs.append((weight_ref.at[pl.ds(start + k * step, step), :], held.at[pl.ds(k * step, step), :]))
        copies = moves(pairs, sems)
        copies[0].wait()
        outs = []
        for k in range(cuts):
            at = pl.ds(k * step, step)
            copies[1 + k].wait()
            out[:, at] = lax.dot_general(
                side[...], held[at, :], ACROSS, preferred_element_type=F32
            ).astype(BF16)
            outs.append(pltpu.make_async_copy(out.at[:, at], out_ref.at[:, at], out_sems.at[k]))
            outs[k].start()
        for copy in outs:
            copy.wait()

    return run(
        kernel,
        (where, left, weight),
        [SMEM, HBM, HBM],
        [shape(rows, half, dtype=BF16)],
        [HBM],
        [
            pltpu.VMEM((rows, width), BF16),
            pltpu.VMEM((half, width), BF16),
            pltpu.VMEM((rows, half), BF16),
            pltpu.SemaphoreType.DMA((1 + cuts,)),
            pltpu.SemaphoreType.DMA((cuts,)),
        ],
        flops=50 * 10**9,
    )[0]


def middle(score, teacher, devices):
    rows, width = teacher.shape

    def kernel(score_ref, teacher_ref, grad_ref, stats_ref, held, target, grad, lines, sems):
        copies = moves([(score_ref, held), (teacher_ref, target)], sems)
        for copy in copies:
            copy.wait()
        score = held[:, pl.ds(0, width)]
        probs = jnp.exp(score)
        advantage = score - target[...].astype(F32)
        mean = jnp.sum(probs * advantage, axis=1, keepdims=True)
        lse = held[:, pl.ds(width, LANES)][:, 0:1]
        block = packed((lse, mean + lse), rows).T[:2]
        for k in range(devices):
            lines[k] = block
        stats_copy = pltpu.make_async_copy(lines, stats_ref, sems.at[2])
        stats_copy.start()
        grad[...] = (probs * (advantage - mean)).astype(BF16)
        grad_copy = pltpu.make_async_copy(grad, grad_ref, sems.at[3])
        grad_copy.start()
        stats_copy.wait()
        grad_copy.wait()

    return run(
        kernel,
        (score, teacher),
        [HBM, HBM],
        [shape(rows, width, dtype=BF16), shape(devices, 2, rows)],
        [HBM, HBM],
        [
            pltpu.VMEM((rows, width + LANES), F32),
            pltpu.VMEM((rows, width), BF16),
            pltpu.VMEM((rows, width), BF16),
            pltpu.VMEM((devices, 2, rows), F32),
            pltpu.SemaphoreType.DMA((4,)),
        ],
        flops=50 * 10**9,
    )


def chip_products(where, lengths, stats, lefts, weight_far, products, counts, sizes):
    ny, nx, nz = sizes
    rows, half = products[0].shape
    width = weight_far.shape[1]
    slot_count = rows // lengths.shape[0]
    cuts = 4
    step = half // cuts

    def kernel(where_ref, lengths_ref, stats_ref, grad_ref, probs_ref, far_ref, near_ref, base_ref, count_ref, out_ref, kl_ref, passed_ref, left, side, held, mine, out, factors, sems, out_sems):
        start = pl.multiple_of(where_ref[0] * half, half)
        pairs = [(grad_ref, left)]
        for k in range(cuts):
            at = pl.ds(k * step, step)
            pairs += [
                (far_ref.at[pl.ds(start + k * step, step), :], held.at[at, :]),
                (near_ref.at[:, at], mine.at[0, :, at]),
                (base_ref.at[:, at], mine.at[1, :, at]),
            ]
        copies = moves(pairs, sems)
        passed_ref[...] = count_ref[...]
        sums = stats_ref[:, 0, :]
        levels = stats_ref[:, 1, :]
        high = jnp.max(sums, axis=0, keepdims=True)
        share = jnp.exp(sums - high)
        whole = jnp.sum(share, axis=0, keepdims=True)
        lse = high + jnp.log(whole)
        level = jnp.sum(share * levels, axis=0, keepdims=True) / whole
        token = lax.broadcasted_iota(jnp.int32, (1, rows), 1)
        live = jnp.zeros((1, rows), F32)
        for k in range(rows // slot_count):
            inside = (token >= k * slot_count) & (token < k * slot_count + lengths_ref[k])
            live = jnp.where(inside, 1.0, live)
        own_rows = kl_ref.shape[0]
        turn = lax.rem(rows - where_ref[1] * own_rows, rows)
        kl = jnp.broadcast_to(live * (level - lse), (8, rows))
        kl_ref[...] = pltpu.roll(kl, turn, 1)[0, :own_rows]
        lines = []
        for k in (2, 3):
            stat = stats_ref[where_ref[k]]
            factor = live * jnp.exp(stat[0:1] - lse)
            lines += [factor, factor * (stat[1:2] - level)]
        factors[...] = turned(lines)
        copies[0].wait()
        side[...] = (
            factors[:, 2:3] * left[...].astype(F32) + factors[:, 3:4] * probs_ref[...].astype(F32)
        ).astype(BF16)
        outs = []
        for k in range(cuts):
            at = pl.ds(k * step, step)
            for j in range(3):
                copies[1 + 3 * k + j].wait()
            value = lax.dot_general(side[...], held[at, :], ACROSS, preferred_element_type=F32)
            for j in range(2):
                value = value + factors[:, j : j + 1] * mine[j, :, at].astype(F32)
            value = value.reshape(ny, nx * nz * 2, own_rows, step)
            each = ny * own_rows
            for x in range(nx):
                for z in range(nz):
                    for c in range(2):
                        spot = (c * nz + z) * nx + x
                        out[pl.ds(spot * each, each), at] = (
                            value[:, (x * nz + z) * 2 + c].reshape(each, step).astype(BF16)
                        )
            outs.append(pltpu.make_async_copy(out.at[:, at], out_ref.at[:, at], out_sems.at[k]))
            outs[k].start()
        for copy in outs:
            copy.wait()

    return run(
        kernel,
        (where, lengths, stats, *lefts, weight_far, *products, *counts),
        [SMEM, SMEM, VMEM, HBM, VMEM] + [HBM] * 3 + [VMEM],
        [shape(rows, half, dtype=BF16), shape(rows // stats.shape[0]), shape(8, LANES)],
        [HBM, VMEM, VMEM],
        [
            pltpu.VMEM((rows, width), BF16),
            pltpu.VMEM((rows, width), BF16),
            pltpu.VMEM((half, width), BF16),
            pltpu.VMEM((2, rows, half), BF16),
            pltpu.VMEM((rows, half), BF16),
            pltpu.VMEM((rows, LANES), F32),
            pltpu.SemaphoreType.DMA((1 + 3 * cuts,)),
            pltpu.SemaphoreType.DMA((cuts,)),
        ],
        limit=48,
    )


def body(student_hidden, head_weight, teacher_logprob, lengths):
    rows, depth = student_hidden.shape
    devices = lax.axis_size(VOCAB)
    own_rows = rows // devices
    seq_devices = lax.axis_size("seq")
    core = lax.axis_index("core").astype(jnp.int32)
    place = lax.axis_index(VOCAB).astype(jnp.int32)
    order = ("core", "z", "x", "y")
    spot = lax.axis_index(order).astype(jnp.int32)
    sibling = spot + (1 - 2 * core) * (devices // 2)
    where = jnp.stack([core, place, spot, sibling])

    def swap(value):
        return lax.ppermute(value, "core", [(0, 1), (1, 0)])

    def across(value, step):
        return lax.ppermute(value, "seq", [(s, (s + step) % seq_devices) for s in range(seq_devices)])

    def whole(value, axes):
        return lax.all_to_all(value, axes, split_axis=0, concat_axis=0, tiled=True)

    teacher = lax.all_to_all(teacher_logprob, VOCAB, split_axis=1, concat_axis=0, tiled=True)
    weight_far = swap(head_weight)
    score, probs, base, count = first_products(where, student_hidden, head_weight, lengths)
    probs_far = swap(probs)

    grad, stats = middle(score, teacher, devices)
    grad_far = swap(grad)
    stats = whole(stats, order)
    near = near_product(where, grad, head_weight)

    chip_sum, token_kl, count = chip_products(
        where,
        lengths,
        stats,
        (grad_far, probs_far),
        weight_far,
        (near, base),
        (count,),
        tuple(lax.axis_size(axis) for axis in ("y", "x", "z")),
    )
    spread = whole(
        chip_sum.reshape(devices, own_rows, depth // 2), order
    )
    count = count + sum(across(count, step) for step in range(1, seq_devices))
    summed = jnp.sum(spread.astype(F32).reshape(2, devices // 2, own_rows, depth // 2), axis=1)
    weight = jnp.broadcast_to((float(rows * seq_devices) / count)[:own_rows, :1], summed.shape[1:])
    rounded = (summed * weight[None]).astype(BF16)
    hidden_grad = jnp.concatenate([rounded[0], rounded[1]], axis=1)
    return hidden_grad, token_kl


def solution(mesh, sizes=(4, 4, 4, 2, 2)):
    return jax.shard_map(
        body,
        mesh=Mesh(mesh.devices.reshape(sizes), ALL),
        in_specs=(P("seq", None), P(None, VOCAB), P(ALL, None), P("seq")),
        out_specs=(P(ALL, None), P(ALL)),
        check_vma=False,
    )
```

```python
import jax
import jax.numpy as jnp
from jax import lax
from jax.experimental import pallas as pl
from jax.experimental.pallas import tpu as pltpu
from jax.sharding import Mesh, PartitionSpec as P

VOCAB = ("y", "x", "z", "core")
ALL = ("seq",) + VOCAB
F32 = jnp.float32
BF16 = jnp.bfloat16
MIB = 2**20
LANES = 128
ACROSS = (((1,), (1,)), ((), ()))


def place_of(memory):
    return pl.BlockSpec(memory_space=memory)


VMEM = place_of(pltpu.VMEM)
HBM = place_of(pltpu.HBM)
SMEM = place_of(pltpu.SMEM)


def shape(*sizes, dtype=F32):
    return jax.ShapeDtypeStruct(sizes, dtype)


def run(kernel, operands, specs, outs, out_specs, scratch=(), limit=62, flops=0):
    return pl.pallas_call(
        kernel,
        out_shape=outs,
        in_specs=specs,
        out_specs=out_specs,
        scratch_shapes=list(scratch),
        compiler_params=pltpu.CompilerParams(vmem_limit_bytes=limit * MIB),
        cost_estimate=pl.CostEstimate(flops=flops, bytes_accessed=0, transcendentals=0),
    )(*operands)


def moves(pairs, sems):
    copies = [pltpu.make_async_copy(a, b, sems.at[k]) for k, (a, b) in enumerate(pairs)]
    for copy in copies:
        copy.start()
    return copies


def packed(columns, rows):
    lane = lax.broadcasted_iota(jnp.int32, (rows, LANES), 1)
    out = jnp.zeros((rows, LANES), F32)
    for k, column in enumerate(columns):
        out = jnp.where(lane == k, column, out)
    return out


def turned(lines):
    rows = lines[0].shape[1]
    return jnp.concatenate(list(lines) + [jnp.zeros((LANES - len(lines), rows), F32)], axis=0).T


def first_products(where, hidden, weight, lengths):
    rows, depth = hidden.shape
    width = weight.shape[1]
    half = depth // 2
    cuts = 4
    step = depth // cuts

    def kernel(where_ref, lengths_ref, hidden_ref, weight_ref, score_ref, probs_ref, base_ref, count_ref, left, held, score, probs, base, sems, out_sems):
        pairs = []
        for k in range(cuts):
            at = pl.ds(k * step, step)
            pairs += [(hidden_ref.at[:, at], left.at[:, at]), (weight_ref.at[at, :], held.at[at, :])]
        copies = moves(pairs, sems)
        total = lengths_ref[0]
        for k in range(1, lengths.shape[0]):
            total = total + lengths_ref[k]
        count_ref[...] = jnp.full(count_ref.shape, total.astype(F32))
        body = pl.ds(0, width)
        for k in range(cuts):
            copies[2 * k].wait()
            copies[2 * k + 1].wait()
            at = pl.ds(k * step, step)
            product = jnp.dot(left[:, at], held[at, :], preferred_element_type=F32)
            if k == 0:
                score[:, body] = product
            else:
                score[:, body] += product
        logits = score[:, body]
        top = jnp.max(logits, axis=1, keepdims=True)
        mass = jnp.exp(logits - top)
        total = jnp.sum(mass, axis=1, keepdims=True)
        probs[...] = (mass * (1.0 / total)).astype(BF16)
        outs = [(probs, probs_ref), (score, score_ref), (base, base_ref)]
        copies = [pltpu.make_async_copy(*pair, out_sems.at[k]) for k, pair in enumerate(outs)]
        copies[0].start()
        lse = top + jnp.log(total)
        score[:, body] = logits - lse
        score[:, pl.ds(width, LANES)] = packed((lse,), rows)
        copies[1].start()
        at = pl.ds(pl.multiple_of(where_ref[0] * half, half), half)
        base[...] = lax.dot_general(
            probs[...], held[at, :], ACROSS, preferred_element_type=F32
        ).astype(BF16)
        copies[2].start()
        for copy in copies:
            copy.wait()

    return run(
        kernel,
        (where, lengths, hidden, weight),
        [SMEM, SMEM, HBM, HBM],
        [
            shape(rows, width + LANES),
            shape(rows, width, dtype=BF16),
            shape(rows, half, dtype=BF16),
            shape(8, LANES),
        ],
        [HBM] * 3 + [VMEM],
        [
            pltpu.VMEM((rows, depth), BF16),
            pltpu.VMEM((depth, width), BF16),
            pltpu.VMEM((rows, width + LANES), F32),
            pltpu.VMEM((rows, width), BF16),
            pltpu.VMEM((rows, half), BF16),
            pltpu.SemaphoreType.DMA((2 * cuts,)),
            pltpu.SemaphoreType.DMA((3,)),
        ],
        flops=200 * 10**9,
    )


def near_product(where, left, weight):
    rows, width = left.shape
    half = weight.shape[0] // 2
    cuts = 4
    step = half // cuts

    def kernel(where_ref, left_ref, weight_ref, out_ref, side, held, out, sems, out_sems):
        start = pl.multiple_of(where_ref[0] * half, half)
        pairs = [(left_ref, side)]
        for k in range(cuts):
            pairs.append((weight_ref.at[pl.ds(start + k * step, step), :], held.at[pl.ds(k * step, step), :]))
        copies = moves(pairs, sems)
        copies[0].wait()
        outs = []
        for k in range(cuts):
            at = pl.ds(k * step, step)
            copies[1 + k].wait()
            out[:, at] = lax.dot_general(
                side[...], held[at, :], ACROSS, preferred_element_type=F32
            ).astype(BF16)
            outs.append(pltpu.make_async_copy(out.at[:, at], out_ref.at[:, at], out_sems.at[k]))
            outs[k].start()
        for copy in outs:
            copy.wait()

    return run(
        kernel,
        (where, left, weight),
        [SMEM, HBM, HBM],
        [shape(rows, half, dtype=BF16)],
        [HBM],
        [
            pltpu.VMEM((rows, width), BF16),
            pltpu.VMEM((half, width), BF16),
            pltpu.VMEM((rows, half), BF16),
            pltpu.SemaphoreType.DMA((1 + cuts,)),
            pltpu.SemaphoreType.DMA((cuts,)),
        ],
        flops=50 * 10**9,
    )[0]


def middle(score, teacher, devices):
    rows, width = teacher.shape

    def kernel(score_ref, teacher_ref, grad_ref, stats_ref, held, target, grad, lines, sems):
        parts = 2
        part = rows // parts
        copies = moves(
            [
                (a.at[pl.ds(k * part, part), :], b.at[pl.ds(k * part, part), :])
                for k in range(parts)
                for a, b in ((score_ref, held), (teacher_ref, target))
            ],
            sems,
        )
        blocks, means = [], []
        for k in range(parts):
            at = pl.ds(k * part, part)
            copies[2 * k].wait()
            copies[2 * k + 1].wait()
            score = held[at, pl.ds(0, width)]
            probs = jnp.exp(score)
            advantage = score - target[at, :].astype(F32)
            mean = jnp.sum(probs * advantage, axis=1, keepdims=True)
            lse = held[at, pl.ds(width, LANES)][:, 0:1]
            blocks.append(packed((lse, mean + lse), part).T[:2])
            grad[at, :] = (probs * (advantage - mean)).astype(BF16)
        block = jnp.concatenate(blocks, axis=1)
        for k in range(devices):
            lines[k] = block
        stats_copy = pltpu.make_async_copy(lines, stats_ref, sems.at[2 * parts])
        stats_copy.start()
        grad_copy = pltpu.make_async_copy(grad, grad_ref, sems.at[2 * parts + 1])
        grad_copy.start()
        stats_copy.wait()
        grad_copy.wait()

    return run(
        kernel,
        (score, teacher),
        [HBM, HBM],
        [shape(rows, width, dtype=BF16), shape(devices, 2, rows)],
        [HBM, HBM],
        [
            pltpu.VMEM((rows, width + LANES), F32),
            pltpu.VMEM((rows, width), BF16),
            pltpu.VMEM((rows, width), BF16),
            pltpu.VMEM((devices, 2, rows), F32),
            pltpu.SemaphoreType.DMA((6,)),
        ],
        flops=50 * 10**9,
    )


def chip_products(where, lengths, stats, lefts, weight_far, products, counts, sizes):
    ny, nx, nz = sizes
    rows, half = products[0].shape
    width = weight_far.shape[1]
    slot_count = rows // lengths.shape[0]
    cuts = 4
    step = half // cuts

    def kernel(where_ref, lengths_ref, stats_ref, grad_ref, probs_ref, far_ref, near_ref, base_ref, count_ref, out_ref, kl_ref, passed_ref, left, side, held, mine, out, factors, sems, out_sems):
        start = pl.multiple_of(where_ref[0] * half, half)
        pairs = [(grad_ref, left)]
        for k in range(cuts):
            at = pl.ds(k * step, step)
            pairs += [
                (far_ref.at[pl.ds(start + k * step, step), :], held.at[at, :]),
                (near_ref.at[:, at], mine.at[0, :, at]),
                (base_ref.at[:, at], mine.at[1, :, at]),
            ]
        copies = moves(pairs, sems)
        passed_ref[...] = count_ref[...]
        sums = stats_ref[:, 0, :]
        levels = stats_ref[:, 1, :]
        high = jnp.max(sums, axis=0, keepdims=True)
        share = jnp.exp(sums - high)
        whole = jnp.sum(share, axis=0, keepdims=True)
        lse = high + jnp.log(whole)
        level = jnp.sum(share * levels, axis=0, keepdims=True) / whole
        token = lax.broadcasted_iota(jnp.int32, (1, rows), 1)
        live = jnp.zeros((1, rows), F32)
        for k in range(rows // slot_count):
            inside = (token >= k * slot_count) & (token < k * slot_count + lengths_ref[k])
            live = jnp.where(inside, 1.0, live)
        own_rows = kl_ref.shape[0]
        turn = lax.rem(rows - where_ref[1] * own_rows, rows)
        kl = jnp.broadcast_to(live * (level - lse), (8, rows))
        kl_ref[...] = pltpu.roll(kl, turn, 1)[0, :own_rows]
        lines = []
        for k in (2, 3):
            stat = stats_ref[where_ref[k]]
            factor = live * jnp.exp(stat[0:1] - lse)
            lines += [factor, factor * (stat[1:2] - level)]
        factors[...] = turned(lines)
        copies[0].wait()
        side[...] = (
            factors[:, 2:3] * left[...].astype(F32) + factors[:, 3:4] * probs_ref[...].astype(F32)
        ).astype(BF16)
        outs = []
        for k in range(cuts):
            at = pl.ds(k * step, step)
            for j in range(3):
                copies[1 + 3 * k + j].wait()
            value = lax.dot_general(side[...], held[at, :], ACROSS, preferred_element_type=F32)
            for j in range(2):
                value = value + factors[:, j : j + 1] * mine[j, :, at].astype(F32)
            value = value.reshape(ny, nx * nz * 2, own_rows, step)
            each = ny * own_rows
            for x in range(nx):
                for z in range(nz):
                    for c in range(2):
                        spot = (c * nz + z) * nx + x
                        out[pl.ds(spot * each, each), at] = (
                            value[:, (x * nz + z) * 2 + c].reshape(each, step).astype(BF16)
                        )
            outs.append(pltpu.make_async_copy(out.at[:, at], out_ref.at[:, at], out_sems.at[k]))
            outs[k].start()
        for copy in outs:
            copy.wait()

    return run(
        kernel,
        (where, lengths, stats, *lefts, weight_far, *products, *counts),
        [SMEM, SMEM, VMEM, HBM, VMEM] + [HBM] * 3 + [VMEM],
        [shape(rows, half, dtype=BF16), shape(rows // stats.shape[0]), shape(8, LANES)],
        [HBM, VMEM, VMEM],
        [
            pltpu.VMEM((rows, width), BF16),
            pltpu.VMEM((rows, width), BF16),
            pltpu.VMEM((half, width), BF16),
            pltpu.VMEM((2, rows, half), BF16),
            pltpu.VMEM((rows, half), BF16),
            pltpu.VMEM((rows, LANES), F32),
            pltpu.SemaphoreType.DMA((1 + 3 * cuts,)),
            pltpu.SemaphoreType.DMA((cuts,)),
        ],
        limit=48,
    )


def body(student_hidden, head_weight, teacher_logprob, lengths):
    rows, depth = student_hidden.shape
    devices = lax.axis_size(VOCAB)
    own_rows = rows // devices
    seq_devices = lax.axis_size("seq")
    core = lax.axis_index("core").astype(jnp.int32)
    place = lax.axis_index(VOCAB).astype(jnp.int32)
    order = ("core", "z", "x", "y")
    spot = lax.axis_index(order).astype(jnp.int32)
    sibling = spot + (1 - 2 * core) * (devices // 2)
    where = jnp.stack([core, place, spot, sibling])

    def swap(value):
        return lax.ppermute(value, "core", [(0, 1), (1, 0)])

    def across(value, step):
        return lax.ppermute(value, "seq", [(s, (s + step) % seq_devices) for s in range(seq_devices)])

    def whole(value, axes):
        return lax.all_to_all(value, axes, split_axis=0, concat_axis=0, tiled=True)

    teacher = lax.all_to_all(teacher_logprob, VOCAB, split_axis=1, concat_axis=0, tiled=True)
    weight_far = swap(head_weight)
    score, probs, base, count = first_products(where, student_hidden, head_weight, lengths)
    probs_far = swap(probs)

    grad, stats = middle(score, teacher, devices)
    grad_far = swap(grad)
    stats = whole(stats, order)
    near = near_product(where, grad, head_weight)

    chip_sum, token_kl, count = chip_products(
        where,
        lengths,
        stats,
        (grad_far, probs_far),
        weight_far,
        (near, base),
        (count,),
        tuple(lax.axis_size(axis) for axis in ("y", "x", "z")),
    )
    spread = whole(
        chip_sum.reshape(devices, own_rows, depth // 2), order
    )
    count = count + sum(across(count, step) for step in range(1, seq_devices))
    summed = jnp.sum(spread.astype(F32).reshape(2, devices // 2, own_rows, depth // 2), axis=1)
    weight = jnp.broadcast_to((float(rows * seq_devices) / count)[:own_rows, :1], summed.shape[1:])
    rounded = (summed * weight[None]).astype(BF16)
    hidden_grad = jnp.concatenate([rounded[0], rounded[1]], axis=1)
    return hidden_grad, token_kl


def solution(mesh, sizes=(4, 4, 4, 2, 2)):
    return jax.shard_map(
        body,
        mesh=Mesh(mesh.devices.reshape(sizes), ALL),
        in_specs=(P("seq", None), P(None, VOCAB), P(ALL, None), P("seq")),
        out_specs=(P(ALL, None), P(ALL)),
        check_vma=False,
    )
```
